256 devices in a mesh: seq: 32 (over z_hi, x, core), chan: 8 (over y, z_lo).
Axes of the slice: x: 4, y: 4, z: 8 (z_hi: 4, z_lo: 2; z = z_hi * 2 + z_lo), core: 2. Of those that a mesh axis runs over, the one named last changes fastest.
Arguments:
- tokens: bfloat16 [20480, 8192], P('seq'), may hold values from -6 to 6
- w_query: bfloat16 [8192, 2048], P('seq', 'chan'), may hold values from -0.0625 to 0.0625
- w_keyval: bfloat16 [8192, 2, 2048], P('seq', None, 'chan'), may hold values from -0.0625 to 0.0625
- short_taps: float32 [3, 3, 2048], P(None, None, 'chan'), may hold values from -3 to 3
- skip_gain: float32 [2048], P('chan'), may hold values from -4 to 4
- decay_rates: float32 [2048, 16], P('chan'), may hold values from 2.4414063e-05 to 0.06
- residues: float32 [2048, 16], P('chan'), may hold values from -0.2 to 0.2
- w_output: bfloat16 [2048, 8192], P('seq', 'chan'), may hold values from -0.125 to 0.125
Outputs:
- mixed: bfloat16 [20480, 8192], P('seq', 'chan')
The draws below stay inside these ranges and needn't reach their ends.
All inputs are finite; a program needn't handle non-finite values.
Results may differ from the reference program's by a relative error of at most 0.0049.
Values may be sent and summed in bfloat16 or wider, within the bound.
A program may use at most 128 MiB of HBM per device.

```python
import math
import jax
import jax.numpy as jnp
from jax import lax

D = 8192
C = 2048
MODES = 16
TOKENS = 20480


def block_levels(key, extent, cuts, smallest, top_value):
    def one(dim, blocks):
        steps = jax.random.uniform(jax.random.fold_in(jax.random.fold_in(key, 6), dim), (blocks,), jnp.float32, smallest / len(cuts), top_value / len(cuts))
        return jnp.repeat(jnp.exp(steps), extent[dim] // blocks).reshape((-1,) + (1,) * (len(extent) - dim - 1))

    factor_of = one(*cuts[0])
    for cut in cuts[1:]:
        factor_of = factor_of * one(*cut)
    return factor_of


def normal_values(key, shape, scale, reach, cuts=(), held_as=jnp.bfloat16):
    entries = scale * jax.random.normal(key, shape, jnp.float32)
    if cuts:
        entries = entries * block_levels(key, shape, cuts, -0.22, 0.18)
    return jnp.clip(entries, -reach, reach).astype(held_as)


def setup_inputs(seed: int = 0) -> dict:
    splits = jax.random.split(jax.random.key(seed), 9)
    return {
        "tokens": normal_values(splits[0], (TOKENS, D), 1.0, 6.0, ((0, 32),)),
        "w_query": normal_values(splits[1], (D, C), D ** -0.5, 0.0625, ((0, 32), (1, 8))),
        "w_keyval": normal_values(splits[2], (D, 2, C), D ** -0.5, 0.0625, ((0, 32), (2, 8))),
        "short_taps": normal_values(splits[3], (3, 3, C), 0.6, 3.0, ((2, 8),), jnp.float32),
        "skip_gain": normal_values(splits[4], (C,), 1.0, 4.0, ((0, 8),), jnp.float32),
        "decay_rates": jnp.clip(jnp.exp(math.log(0.06) - 7.8069405 * jax.random.uniform(splits[5], (C, MODES), jnp.float32) ** block_levels(splits[5], (C, MODES), ((0, 8),), -0.2, 0.2)), 2.441406286379788e-05, 0.06),
        "residues": normal_values(splits[6], (C, MODES), 0.03, 0.2, ((0, 8),), jnp.float32),
        "w_output": normal_values(splits[7], (C, D), C ** -0.5, 0.125, ((0, 32), (1, 8))),
    }


def reference(tokens, w_query, w_keyval, short_taps, skip_gain, decay_rates, residues, w_output):
    proj_q = jnp.dot(tokens, w_query, preferred_element_type=jnp.float32)
    proj_k = jnp.dot(tokens, w_keyval[:, 0, :], preferred_element_type=jnp.float32)
    proj_v = jnp.dot(tokens, w_keyval[:, 1, :], preferred_element_type=jnp.float32)

    def featurize(projected, which):
        first = jnp.pad(projected, ((1, 0), (0, 0)))[:-1]
        second = jnp.pad(projected, ((2, 0), (0, 0)))[:-2]
        return short_taps[0, which] * projected + short_taps[1, which] * first + short_taps[2, which] * second

    query = featurize(proj_q, 0)
    key = featurize(proj_k, 1)
    value = featurize(proj_v, 2)
    mixed_kv = key * value
    group = min(128, C)
    count = C // group
    signal = mixed_kv.T.reshape(count, group, TOKENS)

    def convolve(pieces):
        block, rates_block, weights_block = pieces
        offsets = jnp.arange(TOKENS, dtype=jnp.float32)
        impulse = jnp.zeros_like(block)
        for mode in range(MODES):
            impulse = impulse + weights_block[:, mode:mode + 1] * jnp.exp(-rates_block[:, mode:mode + 1] * offsets)
        length = 2 * TOKENS
        spectrum = jnp.fft.rfft(block, n=length, axis=1) * jnp.fft.rfft(impulse, n=length, axis=1)
        return jnp.fft.irfft(spectrum, n=length, axis=1)[:, :TOKENS]

    folded = lax.map(convolve, (signal, decay_rates.reshape(count, group, MODES), residues.reshape(count, group, MODES)))
    convolved = folded.reshape(C, TOKENS).T + skip_gain * mixed_kv
    gated = (query * convolved).astype(jnp.bfloat16)
    return jnp.dot(gated, w_output, preferred_element_type=jnp.float32).astype(jnp.bfloat16)
```

```python
import functools

import jax
import jax.numpy as jnp
from jax import lax
from jax.experimental import pallas as pl
from jax.experimental.pallas import tpu as pltpu
from jax.sharding import PartitionSpec as P

MESH = pl.DeviceIdType.MESH
F32 = jnp.float32
BF16 = jnp.bfloat16
MODES = 16
ROWS = 640
SUB = ROWS // 8
HEAD = 16
NSEM = 36


def wrap(value, count):
    return lax.rem(value, count)


def near(j):
    return lax.rem((j * (j + 1)) // 2, 4)


def kernel(tok, wkv_in, wq_in, wo_in, taps, skip, rates, resid, out,
           x_all, wkv, wq, wo, acc_kv, acc_q, mkv, conv, scan, e_own, e_sib, c_x, r_z, gate,
           send, recv, esend, erecv, gsend, grecv, lsem, tsem):
    seq, chan = lax.axis_index("seq"), lax.axis_index("chan")
    core, xx, zh = lax.rem(seq, 2), lax.rem(seq // 2, 4), seq // 8
    yy, zl = chan // 2, lax.rem(chan, 2)

    def at(z, x, k):
        return (wrap(z, 4) * 4 + wrap(x, 4)) * 2 + k

    def cat(y, l):
        return wrap(y, 4) * 2 + l

    sib = at(zh, xx, 1 - core)
    xp, xm, xo = at(zh, xx + 1, core), at(zh, xx + 3, core), at(zh, xx + 2, core)
    zp, zm, zo = at(zh + 1, xx, core), at(zh + 3, xx, core), at(zh + 2, xx, core)
    yp, ym, lp = cat(yy + 1, zl), cat(yy + 3, zl), cat(yy, 1 - zl)
    following, before = wrap(seq + 1, 32), wrap(seq + 31, 32)

    def copy(src, dst, s, r, **to):
        return pltpu.make_async_remote_copy(
            src_ref=src, dst_ref=dst, send_sem=s, recv_sem=r, device_id=to, device_id_type=MESH)

    barrier = pltpu.get_barrier_semaphore()
    for to in (sib, xp, xm, xo, zp, zm, zo, before):
        pl.semaphore_signal(barrier, inc=1, device_id={"seq": to}, device_id_type=MESH)
    for to in (yp, ym, lp):
        pl.semaphore_signal(barrier, inc=1, device_id={"chan": to}, device_id_type=MESH)
    load = pltpu.make_async_copy(tok, x_all.at[pl.ds(HEAD, ROWS), :], lsem.at[0])
    load.start()
    pl.semaphore_wait(barrier, 11)

    class Gather:
        def __init__(self, p, src, buf, by_rows):
            self.p, self.src, self.buf, self.by_rows = p, src, buf, by_rows
            self.r, self.n = src.shape

        def piece(self, z, x, k, half=None):
            first = pl.multiple_of(at(z, x, k) * self.r, self.r)
            if half is None:
                return self.buf.at[pl.ds(first, self.r), :]
            if self.by_rows:
                h = self.r // 2
                return self.buf.at[pl.ds(pl.multiple_of(first + half * h, h), h), :]
            h = self.n // 2
            return self.buf.at[pl.ds(first, self.r), pl.ds(half * h, h)]

        def put(self, ref, i, to, src=None):
            copy(ref if src is None else src, ref, send.at[self.p, i], recv.at[self.p, i], seq=to).start()

        def got(self, ref, i):
            copy(ref, ref, send.at[self.p, i], recv.at[self.p, i], seq=sib).wait_recv()

        def start(self):
            own = self.piece(zh, xx, core)
            self.local = pltpu.make_async_copy(self.src, own, lsem.at[1 + self.p])
            self.put(own, 0, zp, self.src)
            self.put(own, 1, zm, self.src)
            self.put(own, 4, xp, self.src)
            self.put(own, 8, xm, self.src)
            self.put(own, 20, sib, self.src)
            self.local.start()

        def spread(self, ref, j):
            self.put(ref, 4 + j, xp)
            self.put(ref, 8 + j, xm)
            self.put(ref, 20 + j, sib)

        def z_near(self):
            ref = self.piece(zh + 3, xx, core)
            self.got(ref, 0)
            self.put(self.piece(zh + 3, xx, core, 0), 2, zp)
            self.spread(ref, 2)
            ref = self.piece(zh + 1, xx, core)
            self.got(ref, 1)
            self.put(self.piece(zh + 1, xx, core, 1), 3, zm)
            self.spread(ref, 1)

        def z_far(self):
            self.got(self.piece(zh + 2, xx, core, 0), 2)
            self.got(self.piece(zh + 2, xx, core, 1), 3)
            self.spread(self.piece(zh + 2, xx, core), 3)

        def x_near(self, j):
            z = zh + near(j)
            ref = self.piece(z, xx + 3, core)
            self.got(ref, 4 + j)
            self.put(self.piece(z, xx + 3, core, 0), 12 + j, xp)
            self.put(ref, 24 + j, sib)
            ref = self.piece(z, xx + 1, core)
            self.got(ref, 8 + j)
            self.put(self.piece(z, xx + 1, core, 1), 16 + j, xm)
            self.put(ref, 28 + j, sib)

        def x_far(self, j):
            z = zh + near(j)
            self.got(self.piece(z, xx + 2, core, 0), 12 + j)
            self.got(self.piece(z, xx + 2, core, 1), 16 + j)
            self.put(self.piece(z, xx + 2, core), 32 + j, sib)

        def other(self, j, dx, c):
            z = zh + near(j)
            self.got(self.piece(z, xx + dx, 1 - core), c + j)

        def drain(self):
            full, half = self.piece(zh, xx, core), self.piece(zh, xx, core, 0)

            def sent(ref, i):
                copy(ref, ref, send.at[self.p, i], recv.at[self.p, i], seq=sib).wait_send()

            for i in (0, 1):
                sent(full, i)
            for i in (2, 3):
                sent(half, i)

            @pl.loop(0, 8)
            def _(i):
                sent(full, 4 + i)
                sent(half, 12 + i)
                sent(full, 20 + i)
                sent(full, 28 + i)

    kv = Gather(0, wkv_in, wkv, True)
    qq = Gather(1, wq_in, wq, True)
    ww = Gather(2, wo_in, wo, False)

    def multiply(g, acc, j, dx, c):
        g.other(j, dx, c)
        first = pl.multiple_of(at(zh + near(j), xx + dx, 0) * g.r, 2 * g.r)
        columns = pl.ds(first, 2 * g.r)
        for n in range(g.n // 256):
            acc[:, n * 256:(n + 1) * 256] += jnp.dot(
                x_all[:, columns], g.buf[columns, n * 256:(n + 1) * 256], preferred_element_type=F32)

    def short(acc, cols, which, lanes, i):
        v = acc[pl.ds(pl.multiple_of(i * SUB + HEAD - 8, 8), SUB + 8), cols]
        return (taps[0, which:which + 1, lanes] * v[8:] + taps[1, which:which + 1, lanes] * v[7:-1]
                + taps[2, which:which + 1, lanes] * v[6:-2])

    rank8 = lax.broadcasted_iota(jnp.int32, (8, 128), 0)

    def wide(row):
        return jnp.broadcast_to(row, (8, 128))

    kv.start()
    tail = copy(tok.at[pl.ds(ROWS - HEAD, HEAD), :], x_all.at[pl.ds(0, HEAD), :], tsem.at[0], tsem.at[1], seq=following)
    tail.start()
    acc_kv[...] = jnp.zeros_like(acc_kv)
    acc_q[...] = jnp.zeros_like(acc_q)
    kv.z_near()
    kv.z_far()
    load.wait()
    tail.wait_recv()
    kv.local.wait()

    @pl.loop(0, 4)
    def _(j):
        kv.x_near(j)
        multiply(kv, acc_kv, j, 0, 20)

    qq.start()

    @pl.loop(0, 4)
    def _(j):
        kv.x_far(j)
        multiply(kv, acc_kv, j, 3, 24)
        multiply(kv, acc_kv, j, 1, 28)

    qq.z_near()
    qq.z_far()
    qq.local.wait()

    @pl.loop(0, 4)
    def _(j):
        multiply(kv, acc_kv, j, 2, 32)

    acc_kv[0:HEAD, :] = jnp.where(seq == 0, 0.0, acc_kv[0:HEAD, :])

    for l in range(2):
        lanes = slice(l * 128, (l + 1) * 128)

        @pl.loop(0, 8)
        def _(i):
            key = short(acc_kv, slice(l * 128, (l + 1) * 128), 1, lanes, i)
            value = short(acc_kv, slice(256 + l * 128, 256 + (l + 1) * 128), 2, lanes, i)
            mkv[pl.ds(pl.multiple_of(l * ROWS + i * SUB, 8), SUB), :] = key * value

    for l in range(2):
        lanes = slice(l * 128, (l + 1) * 128)
        a = [wide(jnp.exp(-rates[m:m + 1, lanes])) for m in range(MODES)]
        r = [wide(resid[m:m + 1, lanes]) for m in range(MODES)]

        def step(t, hs):
            v = mkv[pl.ds(l * ROWS + t, 8, stride=SUB), :]
            hs = [a[m] * hs[m] + v for m in range(MODES)]
            terms = [r[m] * hs[m] for m in range(MODES)]
            while len(terms) > 1:
                terms = [p + q for p, q in zip(terms[::2], terms[1::2])]
            conv[pl.ds(l * ROWS + t, 8, stride=SUB), :] = terms[0]
            return tuple(hs)

        hs = lax.fori_loop(0, SUB, step, (jnp.zeros((8, 128), F32),) * MODES)
        for m in range(MODES):
            v = hs[m]
            for d in (1, 2, 4):
                factor = wide(jnp.exp(-rates[m:m + 1, lanes] * float(SUB * d)))
                v = v + jnp.where(rank8 >= d, factor * pltpu.roll(v, d, 0), 0.0)
            scan[l * MODES + m] = v
            e_own[m:m + 1, lanes] = v[7:8, :]

    def eput(src, dst, i, to):
        copy(src, dst, esend.at[i], erecv.at[i], seq=to).start()

    def egot(ref, i):
        copy(ref, ref, esend.at[i], erecv.at[i], seq=sib).wait_recv()

    eput(e_own, e_sib, 0, sib)

    @pl.loop(0, 4)
    def _(j):
        qq.x_near(j)
        multiply(qq, acc_q, j, 0, 20)

    egot(e_sib, 0)
    lam = rates[...]
    e0 = jnp.where(core == 0, e_own[...], e_sib[...])
    e1 = jnp.where(core == 0, e_sib[...], e_own[...])
    step1 = jnp.exp(-lam * float(ROWS))
    c_x[xx] = step1 * e0 + e1
    eput(c_x.at[xx], c_x.at[xx], 1, xp)
    eput(c_x.at[xx], c_x.at[xx], 2, xo)
    eput(c_x.at[xx], c_x.at[xx], 3, xm)
    ww.start()

    @pl.loop(0, 2)
    def _(j):
        qq.x_far(j)
        multiply(qq, acc_q, j, 3, 24)
        multiply(qq, acc_q, j, 1, 28)

    for d in (1, 2, 3):
        egot(c_x.at[wrap(xx + 4 - d, 4)], d)
    row = c_x[3]
    in_chip = jnp.zeros_like(lam)
    for k in range(4):
        if k < 3:
            row = row + jnp.exp(-lam * float(2 * ROWS * (3 - k))) * c_x[k]
            gap = jnp.maximum(xx - 1 - k, 0).astype(F32) * float(2 * ROWS)
            in_chip = in_chip + jnp.where(k < xx, jnp.exp(-lam * gap) * c_x[k], 0.0)
    r_z[zh] = row
    eput(r_z.at[zh], r_z.at[zh], 4, zp)
    eput(r_z.at[zh], r_z.at[zh], 5, zo)
    eput(r_z.at[zh], r_z.at[zh], 6, zm)
    ww.z_near()

    @pl.loop(2, 4)
    def _(j):
        qq.x_far(j)
        multiply(qq, acc_q, j, 3, 24)
        multiply(qq, acc_q, j, 1, 28)

    ww.z_far()
    for d in (1, 2, 3):
        egot(r_z.at[wrap(zh + 4 - d, 4)], 3 + d)
    in_row = jnp.zeros_like(lam)
    for k in range(3):
        gap = jnp.maximum(zh - 1 - k, 0).astype(F32) * float(8 * ROWS)
        in_row = in_row + jnp.where(k < zh, jnp.exp(-lam * gap) * r_z[k], 0.0)
    in_chip = in_chip + jnp.exp(-lam * (xx.astype(F32) * float(2 * ROWS))) * in_row
    enter = jnp.where(core == 0, in_chip, e0 + step1 * in_chip)

    for l in range(2):
        lanes = slice(l * 128, (l + 1) * 128)
        a = [wide(jnp.exp(-rates[m:m + 1, lanes])) for m in range(MODES)]
        gs = []
        for m in range(MODES):
            rate = wide(rates[m:m + 1, lanes])
            first = jnp.where(rank8 >= 1, pltpu.roll(scan[l * MODES + m], 1, 0), 0.0)
            first = first + jnp.exp(-rate * (rank8.astype(F32) * float(SUB))) * wide(enter[m:m + 1, lanes])
            gs.append(wide(resid[m:m + 1, lanes]) * a[m] * first)
        direct = wide(skip[0:1, lanes])

        def step(t, gs):
            terms = list(gs)
            while len(terms) > 1:
                terms = [p + q for p, q in zip(terms[::2], terms[1::2])]
            place = pl.ds(l * ROWS + t, 8, stride=SUB)
            conv[place, :] = conv[place, :] + terms[0] + direct * mkv[place, :]
            return tuple(a[m] * gs[m] for m in range(MODES))

        lax.fori_loop(0, SUB, step, tuple(gs))

    @pl.loop(0, 2)
    def _(j):
        ww.x_near(j)

    @pl.loop(0, 4)
    def _(j):
        multiply(qq, acc_q, j, 2, 32)

    acc_q[0:HEAD, :] = jnp.where(seq == 0, 0.0, acc_q[0:HEAD, :])

    def gref(c, l, half=None):
        ref = gate.at[c * 2 + l]
        return ref if half is None else ref.at[pl.ds(half * (ROWS // 2), ROWS // 2), :]

    def gput(ref, i, l, to):
        copy(ref, ref, gsend.at[l, i], grecv.at[l, i], chan=to).start()

    def ggot(ref, i, l):
        copy(ref, ref, gsend.at[l, i], grecv.at[l, i], chan=lp).wait_recv()

    for l in range(2):
        lanes = slice(l * 128, (l + 1) * 128)
        mine = gate.at[chan * 2 + l]

        @pl.loop(0, 8)
        def _(i):
            query = short(acc_q, lanes, 0, lanes, i)
            done = query * conv[pl.ds(pl.multiple_of(l * ROWS + i * SUB, 8), SUB), :]
            mine[pl.ds(pl.multiple_of(i * SUB, 16), SUB), :] = done.astype(BF16)

        gput(mine, 0, l, lp)
        gput(mine, 1, l, yp)
        gput(mine, 2, l, ym)

    @pl.loop(2, 4)
    def _(j):
        ww.x_near(j)

    for l in range(2):
        ref = gref(lp, l)
        ggot(ref, 0, l)
        gput(ref, 3, l, yp)
        gput(ref, 4, l, ym)

    for l in range(2):
        for j in range(2):
            side = zl if j == 0 else 1 - zl
            ggot(gref(cat(yy + 3, side), l), 1 + 2 * j, l)
            gput(gref(cat(yy + 3, side), l, 0), 5 + 2 * j, l, yp)
            ggot(gref(cat(yy + 1, side), l), 2 + 2 * j, l)
            gput(gref(cat(yy + 1, side), l, 1), 6 + 2 * j, l, ym)

    @pl.loop(0, 4)
    def _(j):
        ww.x_far(j)

    @pl.loop(0, 4)
    def _(j):
        ww.other(j, 0, 20)
        ww.other(j, 3, 24)
        ww.other(j, 1, 28)
        ww.other(j, 2, 32)

    for l in range(2):
        for j in range(2):
            side = zl if j == 0 else 1 - zl
            ggot(gref(cat(yy + 2, side), l, 0), 5 + 2 * j, l)
            ggot(gref(cat(yy + 2, side), l, 1), 6 + 2 * j, l)
    ww.local.wait()

    @pl.loop(0, out.shape[1] // 256)
    def _(n):
        columns = pl.ds(pl.multiple_of(n * 256, 256), 256)
        whole = jnp.concatenate([gate[i] for i in range(16)], axis=1)
        out[:, columns] = jnp.dot(whole, wo[:, columns], preferred_element_type=F32).astype(BF16)

    for g in (kv, qq, ww):
        g.drain()
    tail.wait_send()
    for i, ref in enumerate([e_own] + [c_x.at[0]] * 3 + [r_z.at[0]] * 3):
        copy(ref, ref, esend.at[i], erecv.at[i], seq=sib).wait_send()
    for l in range(2):
        for i in range(9):
            ref = gref(chan, l, None if i < 5 else 0)
            copy(ref, ref, gsend.at[l, i], grecv.at[l, i], chan=lp).wait_send()


def shards(tokens, w_query, w_keyval, short_taps, skip_gain, decay_rates, residues, w_output):
    depth, _, width = w_keyval.shape
    hbm, vmem = pl.BlockSpec(memory_space=pl.ANY), pl.BlockSpec(memory_space=pltpu.VMEM)
    dma = pltpu.SemaphoreType.DMA
    model = tokens.shape[1]
    return pl.pallas_call(
        kernel,
        out_shape=jax.ShapeDtypeStruct((ROWS, w_output.shape[1]), BF16),
        in_specs=[hbm] * 4 + [vmem] * 4,
        out_specs=vmem,
        scratch_shapes=[
            pltpu.VMEM((HEAD + ROWS, model), BF16),
            pltpu.VMEM((model, 2 * width), BF16),
            pltpu.VMEM((model, width), BF16),
            pltpu.VMEM((8 * width, w_output.shape[1]), BF16),
            pltpu.VMEM((HEAD + ROWS, 2 * width), F32),
            pltpu.VMEM((HEAD + ROWS, width), F32),
            pltpu.VMEM((2 * ROWS, 128), F32),
            pltpu.VMEM((2 * ROWS, 128), F32),
            pltpu.VMEM((2 * MODES, 8, 128), F32),
            pltpu.VMEM((MODES, width), F32),
            pltpu.VMEM((MODES, width), F32),
            pltpu.VMEM((4, MODES, width), F32),
            pltpu.VMEM((4, MODES, width), F32),
            pltpu.VMEM((16, ROWS, 128), BF16),
            dma((3, NSEM)), dma((3, NSEM)),
            dma((7,)), dma((7,)),
            dma((2, 9)), dma((2, 9)),
            dma((4,)), dma((2,)),
        ],
        compiler_params=pltpu.CompilerParams(
            collective_id=0, has_side_effects=True, vmem_limit_bytes=56 * 1024 * 1024),
        cost_estimate=pl.CostEstimate(flops=2 * ROWS * model * 4 * width, bytes_accessed=2 * ROWS * model, transcendentals=0),
    )(tokens, w_keyval.reshape(depth, 2 * width), w_query, w_output, short_taps, skip_gain[None, :],
      decay_rates.T, residues.T)


def solution(mesh):
    return jax.shard_map(
        shards,
        mesh=mesh,
        in_specs=(
            P("seq", None),
            P("seq", "chan"),
            P("seq", None, "chan"),
            P(None, None, "chan"),
            P("chan"),
            P("chan", None),
            P("chan", None),
            P("seq", "chan"),
        ),
        out_specs=P("seq", "chan"),
        check_vma=False,
    )
```

```python
import functools

import jax
import jax.numpy as jnp
from jax import lax
from jax.experimental import pallas as pl
from jax.experimental.pallas import tpu as pltpu
from jax.sharding import PartitionSpec as P

MESH = pl.DeviceIdType.MESH
F32 = jnp.float32
BF16 = jnp.bfloat16
MODES = 16
ROWS = 640
SUB = ROWS // 8
HEAD = 16
CUT = 208
ORDER = (
    "0.T", "0.S", "2.T", "1.T", "0.X1", "3.T", "2.S", "0.Z2", "0.Z1", "2.X1", "0.X2", "2.Z1", "2.Z2", "1.S", "1.X2",
    "0.B0+", "E", "0.A1-", "0.D10", "0.Z3", "2.X2", "1.X1", "0.B1-", "0.A0-", "0.X3", "0.A0+", "2.A0+", "0.A1+",
    "1.Z1", "0.B1+", "0.B0-", "1.Z2", "0.A2-", "0.D11", "0.M0", "1.X3", "0.B2-", "2.A1-", "2.Z3", "0.B2+", "1.A0-",
    "0.A2+", "0.D01", "0.D00", "1.B1-", "2.X3", "3.S", "3.X2", "1.B1+", "0.D21", "2.M0", "3.X1", "1.Z3", "0.D02",
    "1.A1+", "0.D12", "2.B0+", "1.A0+", "2.A1+", "1.B0+", "2.B1-", "1.B0-", "2.B1+", "0.D20", "2.A2+", "0.M1",
    "2.D11", "2.A0-", "2.B2+", "4.T", "1.D00", "1.A1-", "0.D22", "1.M0", "2.D01", "2.B0-", "1.D11", "0.M3", "1.B2+",
    "1.D01", "1.B2-", "2.B2-", "1.A2+", "4.S", "0.M2", "1.D21", "1.A2-", "1.D10", "C0", "2.A2-", "3.B0+", "1.D20",
    "3.B1-", "2.D00", "2.D21", "1.M1", "2.D10", "2.D20", "3.B0-", "3.X3", "E10", "3.Z1", "1.M3", "1.D02", "3.B1+",
    "3.Z2", "2.D12", "1.D22", "2.M1", "1.D12", "E20", "4.X2", "4.X1", "3.A0+", "2.M3", "2.D22", "4.Z2", "1.M2",
    "2.D02", "4.Z1", "C1", "3.Z3", "E30", "2.M2", "GT00", "E11", "3.B2-", "4.B0+", "3.A0-", "3.D01", "3.A1-", "3.D00",
    "4.A1+", "3.A1+", "4.B1+", "GT01", "3.A2-", "3.D10", "3.D20", "3.A2+", "3.B2+", "4.A0-", "4.A0+", "3.M0", "4.Z3",
    "GL00", "3.D21", "GY000-", "4.B0-", "3.D11", "E21", "GY000+", "3.D02", "3.D22", "3.D12", "3.M3", "GL01", "4.X3",
    "3.M1", "4.A1-", "3.M2", "GY001+", "GY010-", "GY001-", "GY010+", "E31", "4.D00", "GT10", "GT11", "GL10", "GL11",
    "GY100-", "GY100+", "4.D10", "4.A2+", "4.B1-", "4.A2-", "4.B2-", "4.B2+", "4.D02", "GY011-", "GY011+", "4.D12",
    "GY101-", "GY110-", "GY101+", "4.D20", "4.D11", "4.D01", "4.D22", "GY110+", "GY111-", "GY111+", "4.D21", "OUT0",
    "OUT1",
)


def wrap(value, count):
    return lax.rem(value, count)


def kernel(tok, wkv_in, wq_in, wo_in, taps_in, skip_in, rates_in, resid_in, out,
           x_all, wa0, wa1, wq0, wq1, wo, acc0, acc1, acc_q, mkv, conv, scan, e_own, e_sib, c_x, r_z, gate, acc_o, ends,
           taps, skip, rates, resid, raw,
           send, recv, esend, erecv, gsend, grecv, lsem, tsem):
    seq, chan = lax.axis_index("seq"), lax.axis_index("chan")
    core, xx, zh = lax.rem(seq, 2), lax.rem(seq // 2, 4), seq // 8
    yy, zl = chan // 2, lax.rem(chan, 2)

    def at(z, x, k):
        return (wrap(z, 4) * 4 + wrap(x, 4)) * 2 + k

    def cat(y, l):
        return wrap(y, 4) * 2 + l

    sib = at(zh, xx, 1 - core)
    xp, xm, xo = at(zh, xx + 1, core), at(zh, xx + 3, core), at(zh, xx + 2, core)
    zp, zm, zo = at(zh + 1, xx, core), at(zh + 3, xx, core), at(zh + 2, xx, core)
    yp, ym, lp = cat(yy + 1, zl), cat(yy + 3, zl), cat(yy, 1 - zl)
    following, before = wrap(seq + 1, 32), wrap(seq + 31, 32)

    def copy(src, dst, s, r, **to):
        return pltpu.make_async_remote_copy(
            src_ref=src, dst_ref=dst, send_sem=s, recv_sem=r, device_id=to, device_id_type=MESH)

    barrier = pltpu.get_barrier_semaphore()
    for to in (sib, xp, xm, xo, zp, zm, zo, before):
        pl.semaphore_signal(barrier, inc=1, device_id={"seq": to}, device_id_type=MESH)
    for to in (yp, ym, lp):
        pl.semaphore_signal(barrier, inc=1, device_id={"chan": to}, device_id_type=MESH)
    load = pltpu.make_async_copy(tok, x_all.at[pl.ds(HEAD, ROWS), :], lsem.at[1])
    small = [pltpu.make_async_copy(src, dst, lsem.at[6 + i]) for i, (src, dst) in enumerate(
        ((taps_in, taps), (skip_in, skip), (rates_in, rates), (resid_in, resid)))]
    pairs_in = pltpu.make_async_copy(wkv_in, raw, lsem.at[0])
    pairs_in.start()
    load.start()
    for c in small:
        c.start()

    pairs_in.wait()
    apart = jnp.swapaxes(raw[...], 0, 1)
    mine = pl.ds(pl.multiple_of(seq * raw.shape[0], raw.shape[0]), raw.shape[0])
    for l, ref in enumerate((wa0, wa1)):
        for which in range(2):
            ref[mine, which * 128:(which + 1) * 128] = apart[which, :, l * 128:(l + 1) * 128]
    pl.semaphore_wait(barrier, 11)

    class Gather:
        def __init__(self, p, src, buf, cut):
            self.p, self.src, self.buf = p, src, buf
            self.r, self.n = (raw.shape[0], buf.shape[1]) if src is None else src.shape
            self.cut = cut

        def piece(self, z, x, k, part="", half=None, flip=0):
            first = pl.multiple_of(at(z, x, k) * self.r, self.r)
            low, high = {"": (0, self.r), "A": (0, self.cut), "B": (self.cut, self.r)}[part]
            columns = slice(None)
            if half is not None and high - low < 32:
                columns = pl.ds(half * (self.n // 2), self.n // 2)
            elif half is not None:
                units = (high - low) // 16
                middle = low + (units // 2 if flip else units - units // 2) * 16
                low, high = ((low, middle), (middle, high))[half]
            return self.buf.at[pl.ds(pl.multiple_of(first + low, 16), high - low), columns]

        def put(self, ref, i, to, src=None):
            copy(ref if src is None else src, ref, send.at[self.p], recv.at[self.p, i], seq=to).start()

        def got(self, ref, i):
            copy(ref, ref, send.at[self.p], recv.at[self.p, i], seq=sib).wait_recv()

        def pair(self, dz, dx):
            self.put(self.piece(zh + dz, xx + dx, core), 24 + dx, sib)

        def S(self):
            own = self.piece(zh, xx, core)
            self.put(own, 0, zp, self.src)
            self.put(own, 1, zm, self.src)

        def T(self):
            own = self.piece(zh, xx, core)
            self.put(own, 3, xp, self.src)
            self.put(own, 4, xm, self.src)
            self.put(own, 24, sib, self.src)
            self.local = None
            if self.src is not None:
                self.local = pltpu.make_async_copy(self.src, own, lsem.at[self.p])
                self.local.start()

        def ring(self, where, base, plus, minus, d, flip):
            if d == 3:
                self.got(where(3), base)
                self.put(where(3, 0, flip), base + 2, plus)
            elif d == 1:
                self.got(where(1), base + 1)
                self.put(where(1, 1, flip), base + 2, minus)
            else:
                self.got(where(2), base + 2)

        def X(self, i):
            d = (3, 1, 2)[i]
            self.ring(lambda d, h=None, f=0: self.piece(zh, xx + d, core, "", h, f), 3, xp, xm, d, 0)
            part = self.piece(zh, xx + d, core, "B")
            self.put(part, 15 + 3 * i, zp)
            self.put(part, 16 + 3 * i, zm)
            self.pair(0, d)

        def Z(self, j):
            d = (3, 1, 2)[j]
            self.ring(lambda d, h=None, f=0: self.piece(zh + d, xx, core, "", h, f), 0, zp, zm, d, 0)
            part = self.piece(zh + d, xx, core, "A")
            self.put(part, 6 + 3 * j, xp)
            self.put(part, 7 + 3 * j, xm)
            self.pair(d, 0)

        def A(self, j, d):
            dz = (3, 1, 2)[j]
            self.ring(lambda d, h=None, f=0: self.piece(zh + dz, xx + d, core, "A", h, f),
                      6 + 3 * j, xp, xm, d, (j + self.p) % 2)

        def B(self, i, d):
            dx = (3, 1, 2)[i]
            self.ring(lambda d, h=None, f=0: self.piece(zh + d, xx + dx, core, "B", h, f),
                      15 + 3 * i, zp, zm, d, (i + self.p) % 2)

        def D(self, j, i):
            dz, dx = (3, 1, 2)[j], (3, 1, 2)[i]
            if dx == 2:
                self.A(j, 2)
            if dz == 2:
                self.B(i, 2)
            self.pair(dz, dx)

        def others(self, dx):
            self.got(self.buf.at[pl.ds(0, 4 * self.r), :], 24 + dx)

        def drain(self):
            ref = self.buf.at[pl.ds(0, 31 * self.r), :]
            copy(ref, ref, send.at[self.p], recv.at[self.p, 0], seq=sib).wait_send()

    cut = wa0.shape[0] // 32 * CUT // 256
    gathers = [
        Gather(0, None, wa0, cut),
        Gather(1, None, wa1, cut),
        Gather(2, wq_in.at[:, pl.ds(0, 128)], wq0, cut),
        Gather(3, wq_in.at[:, pl.ds(128, 128)], wq1, cut),
        Gather(4, wo_in, wo, wo_in.shape[0] // 4 * 3),
    ]
    started = []
    sums = [(acc0, 0), (acc1, 0), (acc_q, 0), (acc_q, 128)]

    def multiply(p, dx):
        g = gathers[p]
        acc, low = sums[p]
        if not started:
            started.append(True)
            take_ends()
        if dx == 0:
            if g.local is not None:
                g.local.wait()
        g.others(dx)

        @pl.loop(0, 4)
        def _(dz):
            first = pl.multiple_of(at(zh + dz, xx + dx, 0) * g.r, 2 * g.r)
            columns = pl.ds(first, 2 * g.r)
            acc[:, low:low + g.n] += jnp.dot(x_all[:, columns], g.buf[columns, :], preferred_element_type=F32)

    def short(acc, cols, which, lanes, i):
        v = acc[pl.ds(pl.multiple_of(i * SUB + HEAD - 8, 8), SUB + 8), cols]
        return (taps[0, which:which + 1, lanes] * v[8:] + taps[1, which:which + 1, lanes] * v[7:-1]
                + taps[2, which:which + 1, lanes] * v[6:-2])

    rank8 = lax.broadcasted_iota(jnp.int32, (8, 128), 0)

    def wide(row):
        return jnp.broadcast_to(row, (8, 128))

    def total(terms):
        while len(terms) > 1:
            terms = [p + q for p, q in zip(terms[::2], terms[1::2])]
        return terms[0]

    def eput(src, dst, l, i, to):
        copy(src, dst, esend.at[l], erecv.at[l, i], seq=to).start()

    def egot(ref, l, i):
        copy(ref, ref, esend.at[l], erecv.at[l, i], seq=sib).wait_recv()

    def states(l):
        lanes = slice(l * 128, (l + 1) * 128)
        acc = sums[l][0]
        acc[0:HEAD, :] = jnp.where(seq == 0, 0.0, acc[0:HEAD, :])

        @pl.loop(0, 8)
        def _(i):
            key = short(acc, slice(0, 128), 1, lanes, i)
            value = short(acc, slice(128, 256), 2, lanes, i)
            mkv[pl.ds(pl.multiple_of(l * ROWS + i * SUB, 8), SUB), :] = key * value

        a = [wide(jnp.exp(-rates[m:m + 1, lanes])) for m in range(MODES)]
        r = [wide(resid[m:m + 1, lanes]) for m in range(MODES)]

        def step(t, hs):
            v = mkv[pl.ds(l * ROWS + t, 8, stride=SUB), :]
            hs = [a[m] * hs[m] + v for m in range(MODES)]
            conv[pl.ds(l * ROWS + t, 8, stride=SUB), :] = total([r[m] * hs[m] for m in range(MODES)])
            return tuple(hs)

        hs = lax.fori_loop(0, SUB, step, (jnp.zeros((8, 128), F32),) * MODES)
        for m in range(MODES):
            v = hs[m]
            for d in (1, 2, 4):
                factor = wide(jnp.exp(-rates[m:m + 1, lanes] * float(SUB * d)))
                v = v + jnp.where(rank8 >= d, factor * pltpu.roll(v, d, 0), 0.0)
            scan[l * MODES + m] = v
            e_own[l, m:m + 1, :] = v[7:8, :]
        eput(e_own.at[l], e_sib.at[l], l, 0, sib)

    def pairs(l):
        lam = rates[:, l * 128:(l + 1) * 128]
        e0 = jnp.where(core == 0, e_own[l], e_sib[l])
        e1 = jnp.where(core == 0, e_sib[l], e_own[l])
        return lam, jnp.exp(-lam * float(ROWS)), e0, e1

    def chip_state(l):
        egot(e_sib.at[l], l, 0)
        lam, step1, e0, e1 = pairs(l)
        c_x[l, xx] = step1 * e0 + e1
        mine = c_x.at[l, xx]
        for to in (xp, xm, xo):
            eput(mine, mine, l, 1, to)

    def row_state(l):
        lam = rates[:, l * 128:(l + 1) * 128]
        egot(c_x.at[l, pl.ds(0, 3)], l, 1)
        row = c_x[l, 3]
        for k in range(3):
            row = row + jnp.exp(-lam * float(2 * ROWS * (3 - k))) * c_x[l, k]
        r_z[l, zh] = row
        mine = r_z.at[l, zh]
        for to in (zp, zm, zo):
            eput(mine, mine, l, 2, to)

    def enter(l):
        lanes = slice(l * 128, (l + 1) * 128)
        lam, step1, e0, e1 = pairs(l)
        egot(r_z.at[l, pl.ds(0, 3)], l, 2)
        state = jnp.zeros_like(lam)
        for k in range(3):
            gap = jnp.maximum(zh - 1 - k, 0).astype(F32) * float(8 * ROWS)
            state = state + jnp.where(k < zh, jnp.exp(-lam * gap) * r_z[l, k], 0.0)
        state = jnp.exp(-lam * (xx.astype(F32) * float(2 * ROWS))) * state
        for k in range(3):
            gap = jnp.maximum(xx - 1 - k, 0).astype(F32) * float(2 * ROWS)
            state = state + jnp.where(k < xx, jnp.exp(-lam * gap) * c_x[l, k], 0.0)
        state = jnp.where(core == 0, state, e0 + step1 * state)

        a = [wide(jnp.exp(-rates[m:m + 1, lanes])) for m in range(MODES)]
        gs = []
        for m in range(MODES):
            rate = wide(rates[m:m + 1, lanes])
            first = jnp.where(rank8 >= 1, pltpu.roll(scan[l * MODES + m], 1, 0), 0.0)
            first = first + jnp.exp(-rate * (rank8.astype(F32) * float(SUB))) * wide(state[m:m + 1, :])
            gs.append(wide(resid[m:m + 1, lanes]) * a[m] * first)
        direct = wide(skip[0:1, lanes])

        def step(t, gs):
            place = pl.ds(l * ROWS + t, 8, stride=SUB)
            conv[place, :] = conv[place, :] + total(list(gs)) + direct * mkv[place, :]
            return tuple(a[m] * gs[m] for m in range(MODES))

        lax.fori_loop(0, SUB, step, tuple(gs))

    def gref(c, l, q, half=None):
        rows = ROWS // 2 if half is None else ROWS // 4
        return gate.at[c * 2 + l, pl.ds(q * (ROWS // 2) + (half or 0) * rows, rows), :]

    def gput(ref, l, q, i, to):
        copy(ref, ref, gsend.at[l], grecv.at[l, q, i], chan=to).start()

    def ggot(ref, l, q, i):
        copy(ref, ref, gsend.at[l], grecv.at[l, q, i], chan=lp).wait_recv()

    def gating(l, q):
        lanes = slice(l * 128, (l + 1) * 128)
        if q == 0:
            acc_q[0:HEAD, lanes] = jnp.where(seq == 0, 0.0, acc_q[0:HEAD, lanes])
        mine = gate.at[chan * 2 + l]

        @pl.loop(4 * q, 4 * q + 4)
        def _(i):
            query = short(acc_q, lanes, 0, lanes, i)
            done = query * conv[pl.ds(pl.multiple_of(l * ROWS + i * SUB, 8), SUB), :]
            mine[pl.ds(pl.multiple_of(i * SUB, 16), SUB), :] = done.astype(BF16)

        ref = gref(chan, l, q)
        gput(ref, l, q, 0, lp)
        gput(ref, l, q, 1, yp)
        gput(ref, l, q, 2, ym)

    def gate_pair(l, q):
        ref = gref(lp, l, q)
        ggot(ref, l, q, 0)
        gput(ref, l, q, 3, yp)
        gput(ref, l, q, 4, ym)

    def gate_ring(l, q, j, d):
        side = zl if j == 0 else 1 - zl
        ref = gref(cat(yy + d, side), l, q)
        if d == 3:
            ggot(ref, l, q, 1 + 2 * j)
            gput(gref(cat(yy + 3, side), l, q, 0), l, q, 5 + j, yp)
        elif d == 1:
            ggot(ref, l, q, 2 + 2 * j)
            gput(gref(cat(yy + 1, side), l, q, 1), l, q, 5 + j, ym)
        else:
            ggot(ref, l, q, 5 + j)

    def project(l):
        if l == 0:
            for dx in range(4):
                gathers[4].others(dx)
            gathers[4].local.wait()
        for q in range(2):
            for j in range(2):
                gate_ring(l, q, j, 2)

        @pl.loop(0, out.shape[1] // 256)
        def _(n):
            columns = pl.ds(pl.multiple_of(n * 256, 256), 256)
            left = jnp.concatenate([gate[2 * i + l] for i in range(8)], axis=1)
            right = jnp.concatenate([wo[i * 256 + l * 128:i * 256 + l * 128 + 128, columns] for i in range(8)], axis=0)
            part = jnp.dot(left, right, preferred_element_type=F32)
            if l == 0:
                acc_o[:, columns] = part
            else:
                out[:, columns] = (acc_o[:, columns] + part).astype(BF16)

    tail = copy(ends.at[0], ends.at[1], tsem.at[0], tsem.at[1], seq=following)
    parts = x_all.shape[1] // 8
    rank16 = lax.broadcasted_iota(jnp.int32, (HEAD, parts), 0)

    def send_ends():
        load.wait()
        for c in small:
            c.wait()
        packed = jnp.zeros((HEAD, parts), F32)
        for i in range(8):
            rows = x_all[ROWS:ROWS + HEAD, i * parts:(i + 1) * parts].astype(F32)
            packed = jnp.where(rank16 // 2 == i, pltpu.roll(rows, (2 * i + 2) % HEAD, 0), packed)
        ends[0] = packed.astype(BF16)
        tail.start()

    def take_ends():
        tail.wait_recv()
        packed = ends[1].astype(F32)
        for i in range(8):
            rows = packed if i == 7 else pltpu.roll(packed, HEAD - 2 - 2 * i, 0)
            x_all[0:HEAD, i * parts:(i + 1) * parts] = rows.astype(BF16)

    acc0[...] = jnp.zeros_like(acc0)
    acc1[...] = jnp.zeros_like(acc1)
    acc_q[...] = jnp.zeros_like(acc_q)

    actions = {"E": send_ends, "C": states, "E1": chip_state, "E2": row_state, "E3": enter,
               "GT": gating, "GL": gate_pair, "OUT": project}
    for name in ORDER:
        if "." not in name:
            if name[:2] == "GY":
                gate_ring(int(name[2]), int(name[3]), int(name[4]), 3 if name[5] == "-" else 1)
            else:
                what = name.rstrip("01")
                if name[:2] in ("E1", "E2", "E3"):
                    what = name[:2]
                actions[what](*[int(c) for c in name[len(what):]])
            continue
        g, what = gathers[int(name[0])], name[2:]
        kind = what[0]
        if kind == "M":
            multiply(g.p, int(what[1]))
        elif kind in "ST":
            getattr(g, kind)()
        elif kind in "XZ":
            getattr(g, kind)(int(what[1]) - 1)
        elif kind == "D":
            g.D(int(what[1]), int(what[2]))
        else:
            getattr(g, kind)(int(what[1]), 3 if what[2] == "-" else 1)

    for g in gathers:
        g.drain()
    tail.wait_send()
    for l in range(2):
        ref = mkv.at[pl.ds(0, 7 * MODES), :]
        copy(ref, ref, esend.at[l], erecv.at[l, 0], seq=sib).wait_send()
        ref = gate.at[pl.ds(0, 7)]
        copy(ref, ref, gsend.at[l], grecv.at[l, 0, 0], chan=lp).wait_send()


def shards(tokens, w_query, w_keyval, short_taps, skip_gain, decay_rates, residues, w_output):
    depth, _, width = w_keyval.shape
    hbm, vmem = pl.BlockSpec(memory_space=pl.ANY), pl.BlockSpec(memory_space=pltpu.VMEM)
    dma = pltpu.SemaphoreType.DMA
    model = tokens.shape[1]
    return pl.pallas_call(
        kernel,
        out_shape=jax.ShapeDtypeStruct((ROWS, w_output.shape[1]), BF16),
        in_specs=[hbm] * 8,
        out_specs=vmem,
        scratch_shapes=[
            pltpu.VMEM((HEAD + ROWS, model), BF16),
            pltpu.VMEM((model, width), BF16),
            pltpu.VMEM((model, width), BF16),
            pltpu.VMEM((model, width // 2), BF16),
            pltpu.VMEM((model, width // 2), BF16),
            pltpu.VMEM((8 * width, w_output.shape[1]), BF16),
            pltpu.VMEM((HEAD + ROWS, width), F32),
            pltpu.VMEM((HEAD + ROWS, width), F32),
            pltpu.VMEM((HEAD + ROWS, width), F32),
            pltpu.VMEM((2 * ROWS, 128), F32),
            pltpu.VMEM((2 * ROWS, 128), F32),
            pltpu.VMEM((2 * MODES, 8, 128), F32),
            pltpu.VMEM((2, MODES, 128), F32),
            pltpu.VMEM((2, MODES, 128), F32),
            pltpu.VMEM((2, 4, MODES, 128), F32),
            pltpu.VMEM((2, 4, MODES, 128), F32),
            pltpu.VMEM((16, ROWS, 128), BF16),
            pltpu.VMEM((ROWS, w_output.shape[1]), F32),
            pltpu.VMEM((2, HEAD, model // 8), BF16),
            pltpu.VMEM((3, 3, width), F32),
            pltpu.VMEM((1, width), F32),
            pltpu.VMEM((MODES, width), F32),
            pltpu.VMEM((MODES, width), F32),
            pltpu.VMEM((depth, 2, width), BF16),
            dma((5,)), dma((5, 28)),
            dma((2,)), dma((2, 3)),
            dma((2,)), dma((2, 2, 7)),
            dma((10,)), dma((2,)),
        ],
        compiler_params=pltpu.CompilerParams(
            collective_id=0, has_side_effects=True, vmem_limit_bytes=56 * 1024 * 1024),
        cost_estimate=pl.CostEstimate(flops=2 * ROWS * model * 4 * width, bytes_accessed=2 * ROWS * model, transcendentals=0),
    )(tokens, w_keyval, w_query, w_output, short_taps, skip_gain[None, :],
      decay_rates.T, residues.T)


def solution(mesh):
    return jax.shard_map(
        shards,
        mesh=mesh,
        in_specs=(
            P("seq", None),
            P("seq", "chan"),
            P("seq", None, "chan"),
            P(None, None, "chan"),
            P("chan"),
            P("chan", None),
            P("chan", None),
            P("seq", "chan"),
        ),
        out_specs=P("seq", "chan"),
        check_vma=False,
    )
```

```python
import functools

import jax
import jax.numpy as jnp
from jax import lax
from jax.experimental import pallas as pl
from jax.experimental.pallas import tpu as pltpu
from jax.sharding import PartitionSpec as P

MESH = pl.DeviceIdType.MESH
F32 = jnp.float32
BF16 = jnp.bfloat16
MODES = 16
ROWS = 640
SUB = ROWS // 8
HEAD = 16
CUT = 208
ORDER = (
    "0.T", "0.S", "2.T", "1.T", "2.S", "0.X2", "3.T", "2.X2", "0.X1", "2.X1", "0.Z2", "0.Z1", "0.X3", "2.Z1", "2.Z2",
    "0.B0-", "E", "0.B1+", "0.B0+", "0.B1-", "2.X3", "1.S", "2.B1+", "0.A1+", "2.B1-", "1.X2", "2.B0-", "0.D11",
    "2.B0+", "0.Z3", "0.A1-", "0.A0+", "2.A0+", "2.D01", "0.B2-", "1.X1", "0.B2+", "0.A0-", "0.D00", "2.A0-", "3.S",
    "3.X1", "2.Z3", "0.D10", "3.X2", "2.D00", "0.D01", "2.A1+", "2.A1-", "0.M0", "2.D11", "0.A2-", "0.D20", "2.M0",
    "0.A2+", "0.D21", "0.D12", "4.T", "0.M3", "1.Z1", "2.D10", "2.A2+", "2.D21", "0.M1", "0.D02", "1.Z2", "1.B1+",
    "2.A2-", "1.X3", "2.B2-", "1.B0+", "2.D02", "3.X3", "0.D22", "2.D20", "2.B2+", "1.B1-", "1.B0-", "2.M1", "3.B1+",
    "3.Z1", "3.Z2", "0.M2", "3.B1-", "3.B0-", "3.B0+", "1.Z3", "C0", "1.A0-", "1.A1+", "1.B2-", "1.B2+", "4.S",
    "2.D22", "1.A1-", "1.A0+", "3.A1+", "2.D12", "1.M0", "1.D01", "1.D00", "3.B2-", "E10", "1.A2-", "3.A1-", "1.D20",
    "1.D10", "3.A0-", "1.A2+", "1.D11", "2.M2", "3.Z3", "1.D21", "3.A0+", "2.M3", "1.D12", "1.D02", "1.M3", "1.D22",
    "E20", "1.M1", "4.X2", "4.Z1", "1.M2", "C1", "E30", "GT00", "3.D01", "3.B2+", "3.A2+", "3.A2-", "3.D21", "3.D20",
    "3.D11", "E11", "3.D00", "GT01", "3.D10", "4.X1", "3.D12", "3.D02", "3.M0", "3.M1", "E21", "3.D22", "4.Z2",
    "4.B1-", "GL00", "GY000+", "3.M3", "GL01", "GY000-", "4.A0+", "4.X3", "3.M2", "GY010-", "GY010+", "E31", "GT10",
    "4.Z3", "4.B0+", "GT11", "4.B2+", "4.B2-", "4.B1+", "4.A1-", "4.B0-", "GY011-", "4.A1+", "4.D01", "GY001+",
    "4.D10", "GL10", "4.A0-", "4.D11", "4.A2-", "GL11", "4.D00", "4.A2+", "4.D21", "GY001-", "4.D12", "GY011+",
    "GY110+", "GY100-", "GY100+", "GY110-", "4.D20", "4.D02", "4.D22", "GY101+", "GY101-", "GY111-", "GY111+", "OUT0",
    "OUT1",
)


def wrap(value, count):
    return lax.rem(value, count)


def kernel(tok, wkv_in, wq_in, wo_in, taps_in, skip_in, rates_in, resid_in, out,
           x_all, wa0, wa1, wq0, wq1, wo, acc0, acc1, acc_q, mkv, conv, scan, e_own, e_sib, c_x, r_z, gate, acc_o, ends,
           taps, skip, rates, resid, raw, held,
           send, recv, esend, erecv, gsend, grecv, lsem, tsem, osem):
    seq, chan = lax.axis_index("seq"), lax.axis_index("chan")
    core, xx, zh = lax.rem(seq, 2), lax.rem(seq // 2, 4), seq // 8
    yy, zl = chan // 2, lax.rem(chan, 2)

    def at(z, x, k):
        return (wrap(z, 4) * 4 + wrap(x, 4)) * 2 + k

    def cat(y, l):
        return wrap(y, 4) * 2 + l

    sib = at(zh, xx, 1 - core)
    xp, xm, xo = at(zh, xx + 1, core), at(zh, xx + 3, core), at(zh, xx + 2, core)
    zp, zm, zo = at(zh + 1, xx, core), at(zh + 3, xx, core), at(zh + 2, xx, core)
    yp, ym, lp = cat(yy + 1, zl), cat(yy + 3, zl), cat(yy, 1 - zl)
    following, before = wrap(seq + 1, 32), wrap(seq + 31, 32)

    def copy(src, dst, s, r, **to):
        return pltpu.make_async_remote_copy(
            src_ref=src, dst_ref=dst, send_sem=s, recv_sem=r, device_id=to, device_id_type=MESH)

    barrier = pltpu.get_barrier_semaphore()
    for to in (sib, xp, xm, xo, zp, zm, zo, before):
        pl.semaphore_signal(barrier, inc=1, device_id={"seq": to}, device_id_type=MESH)
    for to in (yp, ym, lp):
        pl.semaphore_signal(barrier, inc=1, device_id={"chan": to}, device_id_type=MESH)
    load = pltpu.make_async_copy(tok, x_all.at[pl.ds(HEAD, ROWS), :], lsem.at[1])
    small = [pltpu.make_async_copy(src, dst, lsem.at[6 + i]) for i, (src, dst) in enumerate(
        ((taps_in, taps), (skip_in, skip), (rates_in, rates), (resid_in, resid)))]
    pairs_in = pltpu.make_async_copy(wkv_in, raw, lsem.at[0])
    pairs_in.start()
    load.start()
    for c in small:
        c.start()

    pairs_in.wait()
    apart = jnp.swapaxes(raw[...], 0, 1)
    mine = pl.ds(pl.multiple_of(seq * raw.shape[0], raw.shape[0]), raw.shape[0])
    for l, ref in enumerate((wa0, wa1)):
        for which in range(2):
            ref[mine, which * 128:(which + 1) * 128] = apart[which, :, l * 128:(l + 1) * 128]
    pl.semaphore_wait(barrier, 11)

    class Gather:
        def __init__(self, p, src, buf, cut):
            self.p, self.src, self.buf = p, src, buf
            self.r, self.n = (raw.shape[0], buf.shape[1]) if src is None else src.shape
            self.cut = cut

        def piece(self, z, x, k, part="", half=None, flip=0):
            first = pl.multiple_of(at(z, x, k) * self.r, self.r)
            low, high = {"": (0, self.r), "A": (0, self.cut), "B": (self.cut, self.r)}[part]
            columns = slice(None)
            if half is not None and high - low < 32:
                columns = pl.ds(half * (self.n // 2), self.n // 2)
            elif half is not None:
                units = (high - low) // 16
                middle = low + (units // 2 if flip else units - units // 2) * 16
                low, high = ((low, middle), (middle, high))[half]
            return self.buf.at[pl.ds(pl.multiple_of(first + low, 16), high - low), columns]

        def put(self, ref, i, to, src=None):
            copy(ref if src is None else src, ref, send.at[self.p], recv.at[self.p, i], seq=to).start()

        def got(self, ref, i):
            copy(ref, ref, send.at[self.p], recv.at[self.p, i], seq=sib).wait_recv()

        def pair(self, dz, dx):
            self.put(self.piece(zh + dz, xx + dx, core), 24 + dx, sib)

        def S(self):
            own = self.piece(zh, xx, core)
            self.put(own, 0, zp, self.src)
            self.put(own, 1, zm, self.src)

        def T(self):
            own = self.piece(zh, xx, core)
            self.put(own, 3, xp, self.src)
            self.put(own, 4, xm, self.src)
            self.put(own, 24, sib, self.src)
            self.local = None
            if self.src is not None:
                self.local = pltpu.make_async_copy(self.src, own, lsem.at[self.p])
                self.local.start()

        def ring(self, where, base, plus, minus, d, flip):
            if d == 3:
                self.got(where(3), base)
                self.put(where(3, 0, flip), base + 2, plus)
            elif d == 1:
                self.got(where(1), base + 1)
                self.put(where(1, 1, flip), base + 2, minus)
            else:
                self.got(where(2), base + 2)

        def X(self, i):
            d = (3, 1, 2)[i]
            self.ring(lambda d, h=None, f=0: self.piece(zh, xx + d, core, "", h, f), 3, xp, xm, d, 0)
            part = self.piece(zh, xx + d, core, "B")
            self.put(part, 15 + 3 * i, zp)
            self.put(part, 16 + 3 * i, zm)
            self.pair(0, d)

        def Z(self, j):
            d = (3, 1, 2)[j]
            self.ring(lambda d, h=None, f=0: self.piece(zh + d, xx, core, "", h, f), 0, zp, zm, d, 0)
            part = self.piece(zh + d, xx, core, "A")
            self.put(part, 6 + 3 * j, xp)
            self.put(part, 7 + 3 * j, xm)
            self.pair(d, 0)

        def A(self, j, d):
            dz = (3, 1, 2)[j]
            self.ring(lambda d, h=None, f=0: self.piece(zh + dz, xx + d, core, "A", h, f),
                      6 + 3 * j, xp, xm, d, (j + self.p) % 2)

        def B(self, i, d):
            dx = (3, 1, 2)[i]
            self.ring(lambda d, h=None, f=0: self.piece(zh + d, xx + dx, core, "B", h, f),
                      15 + 3 * i, zp, zm, d, (i + self.p) % 2)

        def D(self, j, i):
            dz, dx = (3, 1, 2)[j], (3, 1, 2)[i]
            if dx == 2:
                self.A(j, 2)
            if dz == 2:
                self.B(i, 2)
            self.pair(dz, dx)

        def others(self, dx):
            self.got(self.buf.at[pl.ds(0, 4 * self.r), :], 24 + dx)

        def drain(self):
            ref = self.buf.at[pl.ds(0, 31 * self.r), :]
            copy(ref, ref, send.at[self.p], recv.at[self.p, 0], seq=sib).wait_send()

    cut = wa0.shape[0] // 32 * CUT // 256
    gathers = [
        Gather(0, None, wa0, cut),
        Gather(1, None, wa1, cut),
        Gather(2, wq_in.at[:, pl.ds(0, 128)], wq0, cut),
        Gather(3, wq_in.at[:, pl.ds(128, 128)], wq1, cut),
        Gather(4, wo_in, wo, wo_in.shape[0] // 4 * 3),
    ]
    started = []
    sums = [(acc0, 0), (acc1, 0), (acc_q, 0), (acc_q, 128)]

    def multiply(p, dx):
        g = gathers[p]
        acc, low = sums[p]
        if not started:
            started.append(True)
            take_ends()
        if dx == 0:
            if g.local is not None:
                g.local.wait()
        g.others(dx)

        @pl.loop(0, 4, step=2)
        def _(dz):
            where = [pl.ds(pl.multiple_of(at(zh + dz + i, xx + dx, 0) * g.r, 2 * g.r), 2 * g.r) for i in range(2)]
            left = jnp.concatenate([x_all[:, w] for w in where], axis=1)
            right = jnp.concatenate([g.buf[w, :] for w in where], axis=0)
            acc[:, low:low + g.n] += jnp.dot(left, right, preferred_element_type=F32)

    def short(acc, cols, which, lanes, i):
        v = acc[pl.ds(pl.multiple_of(i * SUB + HEAD - 8, 8), SUB + 8), cols]
        return (taps[0, which:which + 1, lanes] * v[8:] + taps[1, which:which + 1, lanes] * v[7:-1]
                + taps[2, which:which + 1, lanes] * v[6:-2])

    rank8 = lax.broadcasted_iota(jnp.int32, (8, 128), 0)

    def wide(row):
        return jnp.broadcast_to(row, (8, 128))

    def total(terms):
        while len(terms) > 1:
            terms = [p + q for p, q in zip(terms[::2], terms[1::2])]
        return terms[0]

    def eput(src, dst, l, i, to):
        copy(src, dst, esend.at[l], erecv.at[l, i], seq=to).start()

    def egot(ref, l, i):
        copy(ref, ref, esend.at[l], erecv.at[l, i], seq=sib).wait_recv()

    def states(l):
        lanes = slice(l * 128, (l + 1) * 128)
        acc = sums[l][0]
        acc[0:HEAD, :] = jnp.where(seq == 0, 0.0, acc[0:HEAD, :])

        @pl.loop(0, 8)
        def _(i):
            key = short(acc, slice(0, 128), 1, lanes, i)
            value = short(acc, slice(128, 256), 2, lanes, i)
            mkv[pl.ds(pl.multiple_of(l * ROWS + i * SUB, 8), SUB), :] = key * value

        a = [wide(jnp.exp(-rates[m:m + 1, lanes])) for m in range(MODES)]
        r = [wide(resid[m:m + 1, lanes]) for m in range(MODES)]

        def step(t, hs):
            v = mkv[pl.ds(l * ROWS + t, 8, stride=SUB), :]
            hs = [a[m] * hs[m] + v for m in range(MODES)]
            conv[pl.ds(l * ROWS + t, 8, stride=SUB), :] = total([r[m] * hs[m] for m in range(MODES)])
            return tuple(hs)

        hs = lax.fori_loop(0, SUB, step, (jnp.zeros((8, 128), F32),) * MODES)
        for m in range(MODES):
            v = hs[m]
            for d in (1, 2, 4):
                factor = wide(jnp.exp(-rates[m:m + 1, lanes] * float(SUB * d)))
                v = v + jnp.where(rank8 >= d, factor * pltpu.roll(v, d, 0), 0.0)
            scan[l * MODES + m] = v
            e_own[l, m:m + 1, :] = v[7:8, :]
        eput(e_own.at[l], e_sib.at[l], l, 0, sib)

    def pairs(l):
        lam = rates[:, l * 128:(l + 1) * 128]
        e0 = jnp.where(core == 0, e_own[l], e_sib[l])
        e1 = jnp.where(core == 0, e_sib[l], e_own[l])
        return lam, jnp.exp(-lam * float(ROWS)), e0, e1

    def chip_state(l):
        egot(e_sib.at[l], l, 0)
        lam, step1, e0, e1 = pairs(l)
        c_x[l, xx] = step1 * e0 + e1
        mine = c_x.at[l, xx]
        for to in (xp, xm, xo):
            eput(mine, mine, l, 1, to)

    def row_state(l):
        lam = rates[:, l * 128:(l + 1) * 128]
        egot(c_x.at[l, pl.ds(0, 3)], l, 1)
        row = c_x[l, 3]
        for k in range(3):
            row = row + jnp.exp(-lam * float(2 * ROWS * (3 - k))) * c_x[l, k]
        r_z[l, zh] = row
        mine = r_z.at[l, zh]
        for to in (zp, zm, zo):
            eput(mine, mine, l, 2, to)

    def enter(l):
        lanes = slice(l * 128, (l + 1) * 128)
        lam, step1, e0, e1 = pairs(l)
        egot(r_z.at[l, pl.ds(0, 3)], l, 2)
        state = jnp.zeros_like(lam)
        for k in range(3):
            gap = jnp.maximum(zh - 1 - k, 0).astype(F32) * float(8 * ROWS)
            state = state + jnp.where(k < zh, jnp.exp(-lam * gap) * r_z[l, k], 0.0)
        state = jnp.exp(-lam * (xx.astype(F32) * float(2 * ROWS))) * state
        for k in range(3):
            gap = jnp.maximum(xx - 1 - k, 0).astype(F32) * float(2 * ROWS)
            state = state + jnp.where(k < xx, jnp.exp(-lam * gap) * c_x[l, k], 0.0)
        state = jnp.where(core == 0, state, e0 + step1 * state)

        a = [wide(jnp.exp(-rates[m:m + 1, lanes])) for m in range(MODES)]
        gs = []
        for m in range(MODES):
            rate = wide(rates[m:m + 1, lanes])
            first = jnp.where(rank8 >= 1, pltpu.roll(scan[l * MODES + m], 1, 0), 0.0)
            first = first + jnp.exp(-rate * (rank8.astype(F32) * float(SUB))) * wide(state[m:m + 1, :])
            gs.append(wide(resid[m:m + 1, lanes]) * a[m] * first)
        direct = wide(skip[0:1, lanes])

        def step(t, gs):
            place = pl.ds(l * ROWS + t, 8, stride=SUB)
            conv[place, :] = conv[place, :] + total(list(gs)) + direct * mkv[place, :]
            return tuple(a[m] * gs[m] for m in range(MODES))

        lax.fori_loop(0, SUB, step, tuple(gs))

    def gref(c, l, q, half=None):
        rows = ROWS // 2 if half is None else ROWS // 4
        return gate.at[c * 2 + l, pl.ds(q * (ROWS // 2) + (half or 0) * rows, rows), :]

    def gput(ref, l, q, i, to):
        copy(ref, ref, gsend.at[l], grecv.at[l, q, i], chan=to).start()

    def ggot(ref, l, q, i):
        copy(ref, ref, gsend.at[l], grecv.at[l, q, i], chan=lp).wait_recv()

    def gating(l, q):
        lanes = slice(l * 128, (l + 1) * 128)
        if q == 0:
            acc_q[0:HEAD, lanes] = jnp.where(seq == 0, 0.0, acc_q[0:HEAD, lanes])
        mine = gate.at[chan * 2 + l]

        @pl.loop(4 * q, 4 * q + 4)
        def _(i):
            query = short(acc_q, lanes, 0, lanes, i)
            done = query * conv[pl.ds(pl.multiple_of(l * ROWS + i * SUB, 8), SUB), :]
            mine[pl.ds(pl.multiple_of(i * SUB, 16), SUB), :] = done.astype(BF16)

        ref = gref(chan, l, q)
        gput(ref, l, q, 0, lp)
        gput(ref, l, q, 1, yp)
        gput(ref, l, q, 2, ym)

    def gate_pair(l, q):
        ref = gref(lp, l, q)
        ggot(ref, l, q, 0)
        gput(ref, l, q, 3, yp)
        gput(ref, l, q, 4, ym)

    def gate_ring(l, q, j, d):
        side = zl if j == 0 else 1 - zl
        ref = gref(cat(yy + d, side), l, q)
        if d == 3:
            ggot(ref, l, q, 1 + 2 * j)
            gput(gref(cat(yy + 3, side), l, q, 0), l, q, 5 + j, yp)
        elif d == 1:
            ggot(ref, l, q, 2 + 2 * j)
            gput(gref(cat(yy + 1, side), l, q, 1), l, q, 5 + j, ym)
        else:
            ggot(ref, l, q, 5 + j)

    def project(l):
        if l == 0:
            for dx in range(4):
                gathers[4].others(dx)
            gathers[4].local.wait()
        for q in range(2):
            for j in range(2):
                gate_ring(l, q, j, 2)

        @pl.loop(0, out.shape[1] // 256)
        def _(n):
            columns = pl.ds(pl.multiple_of(n * 256, 256), 256)
            left = jnp.concatenate([gate[2 * i + l] for i in range(8)], axis=1)
            right = jnp.concatenate([wo[i * 256 + l * 128:i * 256 + l * 128 + 128, columns] for i in range(8)], axis=0)
            part = jnp.dot(left, right, preferred_element_type=F32)
            if l == 0:
                acc_o[:, columns] = part
            else:
                held[:, columns] = (acc_o[:, columns] + part).astype(BF16)
                pltpu.make_async_copy(held.at[:, columns], out.at[:, columns], osem.at[n]).start()

    tail = copy(ends.at[0], ends.at[1], tsem.at[0], tsem.at[1], seq=following)
    parts = x_all.shape[1] // 8
    rank16 = lax.broadcasted_iota(jnp.int32, (HEAD, parts), 0)

    def send_ends():
        load.wait()
        for c in small:
            c.wait()
        packed = jnp.zeros((HEAD, parts), F32)
        for i in range(8):
            rows = x_all[ROWS:ROWS + HEAD, i * parts:(i + 1) * parts].astype(F32)
            packed = jnp.where(rank16 // 2 == i, pltpu.roll(rows, (2 * i + 2) % HEAD, 0), packed)
        ends[0] = packed.astype(BF16)
        tail.start()

    def take_ends():
        tail.wait_recv()
        packed = ends[1].astype(F32)
        for i in range(8):
            rows = packed if i == 7 else pltpu.roll(packed, HEAD - 2 - 2 * i, 0)
            x_all[0:HEAD, i * parts:(i + 1) * parts] = rows.astype(BF16)

    acc0[...] = jnp.zeros_like(acc0)
    acc1[...] = jnp.zeros_like(acc1)
    acc_q[...] = jnp.zeros_like(acc_q)

    actions = {"E": send_ends, "C": states, "E1": chip_state, "E2": row_state, "E3": enter,
               "GT": gating, "GL": gate_pair, "OUT": project}
    for name in ORDER:
        if "." not in name:
            if name[:2] == "GY":
                gate_ring(int(name[2]), int(name[3]), int(name[4]), 3 if name[5] == "-" else 1)
            else:
                what = name.rstrip("01")
                if name[:2] in ("E1", "E2", "E3"):
                    what = name[:2]
                actions[what](*[int(c) for c in name[len(what):]])
            continue
        g, what = gathers[int(name[0])], name[2:]
        kind = what[0]
        if kind == "M":
            multiply(g.p, int(what[1]))
        elif kind in "ST":
            getattr(g, kind)()
        elif kind in "XZ":
            getattr(g, kind)(int(what[1]) - 1)
        elif kind == "D":
            g.D(int(what[1]), int(what[2]))
        else:
            getattr(g, kind)(int(what[1]), 3 if what[2] == "-" else 1)

    for g in gathers:
        g.drain()
    tail.wait_send()

    @pl.loop(0, out.shape[1] // 256)
    def _(n):
        columns = pl.ds(pl.multiple_of(n * 256, 256), 256)
        pltpu.make_async_copy(held.at[:, columns], out.at[:, columns], osem.at[n]).wait()

    for l in range(2):
        ref = mkv.at[pl.ds(0, 7 * MODES), :]
        copy(ref, ref, esend.at[l], erecv.at[l, 0], seq=sib).wait_send()
        ref = gate.at[pl.ds(0, 7)]
        copy(ref, ref, gsend.at[l], grecv.at[l, 0, 0], chan=lp).wait_send()


def shards(tokens, w_query, w_keyval, short_taps, skip_gain, decay_rates, residues, w_output):
    depth, _, width = w_keyval.shape
    hbm = pl.BlockSpec(memory_space=pl.ANY)
    dma = pltpu.SemaphoreType.DMA
    model = tokens.shape[1]
    return pl.pallas_call(
        kernel,
        out_shape=jax.ShapeDtypeStruct((ROWS, w_output.shape[1]), BF16),
        in_specs=[hbm] * 8,
        out_specs=hbm,
        scratch_shapes=[
            pltpu.VMEM((HEAD + ROWS, model), BF16),
            pltpu.VMEM((model, width), BF16),
            pltpu.VMEM((model, width), BF16),
            pltpu.VMEM((model, width // 2), BF16),
            pltpu.VMEM((model, width // 2), BF16),
            pltpu.VMEM((8 * width, w_output.shape[1]), BF16),
            pltpu.VMEM((HEAD + ROWS, width), F32),
            pltpu.VMEM((HEAD + ROWS, width), F32),
            pltpu.VMEM((HEAD + ROWS, width), F32),
            pltpu.VMEM((2 * ROWS, 128), F32),
            pltpu.VMEM((2 * ROWS, 128), F32),
            pltpu.VMEM((2 * MODES, 8, 128), F32),
            pltpu.VMEM((2, MODES, 128), F32),
            pltpu.VMEM((2, MODES, 128), F32),
            pltpu.VMEM((2, 4, MODES, 128), F32),
            pltpu.VMEM((2, 4, MODES, 128), F32),
            pltpu.VMEM((16, ROWS, 128), BF16),
            pltpu.VMEM((ROWS, w_output.shape[1]), F32),
            pltpu.VMEM((2, HEAD, model // 8), BF16),
            pltpu.VMEM((3, 3, width), F32),
            pltpu.VMEM((1, width), F32),
            pltpu.VMEM((MODES, width), F32),
            pltpu.VMEM((MODES, width), F32),
            pltpu.VMEM((depth, 2, width), BF16),
            pltpu.VMEM((ROWS, w_output.shape[1]), BF16),
            dma((5,)), dma((5, 28)),
            dma((2,)), dma((2, 3)),
            dma((2,)), dma((2, 2, 7)),
            dma((10,)), dma((2,)), dma((4,)),
        ],
        compiler_params=pltpu.CompilerParams(
            collective_id=0, has_side_effects=True, vmem_limit_bytes=56 * 1024 * 1024),
        cost_estimate=pl.CostEstimate(flops=2 * ROWS * model * 4 * width, bytes_accessed=2 * ROWS * model, transcendentals=0),
    )(tokens, w_keyval, w_query, w_output, short_taps, skip_gain[None, :],
      decay_rates.T, residues.T)


def solution(mesh):
    return jax.shard_map(
        shards,
        mesh=mesh,
        in_specs=(
            P("seq", None),
            P("seq", "chan"),
            P("seq", None, "chan"),
            P(None, None, "chan"),
            P("chan"),
            P("chan", None),
            P("chan", None),
            P("seq", "chan"),
        ),
        out_specs=P("seq", "chan"),
        check_vma=False,
    )
```

```python
import functools

import jax
import jax.numpy as jnp
from jax import lax
from jax.experimental import pallas as pl
from jax.experimental.pallas import tpu as pltpu
from jax.sharding import PartitionSpec as P

MESH = pl.DeviceIdType.MESH
F32 = jnp.float32
BF16 = jnp.bfloat16
MODES = 16
ROWS = 640
SUB = ROWS // 8
HEAD = 16
CUT = 224
CUT_KV = 224
ORDER = (
    "2.T", "2.S", "3.T", "RL", "0.T", "0.S", "1.T", "2.X2", "2.Z1", "2.Z2", "0.X1", "2.X1", "0.X2", "E", "0.Z2",
    "0.Z1", "2.Z3", "2.A0-", "2.B1+", "2.A0+", "2.B1-", "2.X3", "2.B0-", "2.A1-", "0.B1+", "0.B1-", "0.X3", "2.B0+",
    "2.D01", "1.S", "2.M0", "1.X2", "0.Z3", "0.A1-", "0.B0+", "0.A1+", "0.B0-", "2.D10", "2.B2+", "2.A1+", "3.S",
    "2.D11", "3.X2", "0.D11", "2.B2-", "2.D00", "0.D10", "3.X1", "0.B2-", "0.B2+", "1.X1", "0.A0-", "2.A2+", "2.D02",
    "2.D21", "0.A0+", "2.A2-", "2.D20", "0.D00", "0.M0", "2.M3", "0.D01", "0.A2+", "0.A2-", "0.D21", "1.Z1", "1.Z2",
    "0.D20", "2.M1", "0.D12", "3.X3", "1.B1+", "4.T", "0.D02", "0.M1", "0.D22", "1.B1-", "1.X3", "1.B0+", "1.B0-",
    "2.D12", "4.S", "0.M3", "2.D22", "1.Z3", "0.M2", "C0", "1.A1+", "1.A0+", "3.B1-", "1.A0-", "1.D11", "1.A1-",
    "2.M2", "3.B2-", "3.B0+", "3.B1+", "1.D10", "1.B2+", "3.B0-", "1.D01", "1.B2-", "1.D00", "E10", "1.A2-", "1.A2+",
    "1.D21", "3.Z1", "3.Z2", "1.D20", "1.M0", "4.X2", "4.X1", "1.D02", "1.M1", "1.D12", "E20", "1.D22", "3.B2+",
    "1.M3", "3.Z3", "4.Z1", "3.A1+", "3.D11", "3.A0+", "3.A0-", "3.D01", "1.M2", "C1", "3.A1-", "E30", "GT00",
    "3.A2-", "3.A2+", "3.D21", "E11", "GT01", "3.M0", "3.D10", "3.D20", "3.D00", "3.D02", "3.M1", "E21", "3.D22",
    "4.Z2", "3.D12", "GL00", "GY000+", "3.M3", "GL01", "GY000-", "GY010+", "4.X3", "GY010-", "3.M2", "E31", "GT10",
    "4.Z3", "GT11", "4.B1-", "4.B0-", "4.B1+", "GY001+", "4.B0+", "4.A1+", "4.A0-", "4.A1-", "4.D11", "GY001-",
    "4.A0+", "4.B2-", "GL10", "4.B2+", "4.D01", "4.A2+", "4.A2-", "GL11", "GY011+", "4.D00", "4.D20", "GY011-",
    "GY110+", "4.D10", "4.D12", "4.D02", "4.D21", "GY110-", "GY100-", "GY100+", "4.D22", "GY111+", "GY111-", "GY101-",
    "GY101+", "OUT0", "OUT1",
)


def wrap(value, count):
    return lax.rem(value, count)


def kernel(tok, wkv_in, wq_in, wo_in, taps_in, skip_in, rates_in, resid_in, out,
           x_all, wa0, wa1, wq0, wq1, wo, acc0, acc1, acc_q, mkv, conv, scan, e_own, e_sib, c_x, r_z, gate, acc_o, ends,
           taps, skip, rates, resid, raw, held,
           send, recv, esend, erecv, gsend, grecv, lsem, tsem, osem):
    seq, chan = lax.axis_index("seq"), lax.axis_index("chan")
    core, xx, zh = lax.rem(seq, 2), lax.rem(seq // 2, 4), seq // 8
    yy, zl = chan // 2, lax.rem(chan, 2)

    def at(z, x, k):
        return (wrap(z, 4) * 4 + wrap(x, 4)) * 2 + k

    def cat(y, l):
        return wrap(y, 4) * 2 + l

    sib = at(zh, xx, 1 - core)
    xp, xm, xo = at(zh, xx + 1, core), at(zh, xx + 3, core), at(zh, xx + 2, core)
    zp, zm, zo = at(zh + 1, xx, core), at(zh + 3, xx, core), at(zh + 2, xx, core)
    yp, ym, lp = cat(yy + 1, zl), cat(yy + 3, zl), cat(yy, 1 - zl)
    following, before = wrap(seq + 1, 32), wrap(seq + 31, 32)

    def copy(src, dst, s, r, **to):
        return pltpu.make_async_remote_copy(
            src_ref=src, dst_ref=dst, send_sem=s, recv_sem=r, device_id=to, device_id_type=MESH)

    barrier = pltpu.get_barrier_semaphore()
    for to in (sib, xp, xm, xo, zp, zm, zo, before):
        pl.semaphore_signal(barrier, inc=1, device_id={"seq": to}, device_id_type=MESH)
    for to in (yp, ym, lp):
        pl.semaphore_signal(barrier, inc=1, device_id={"chan": to}, device_id_type=MESH)
    load = pltpu.make_async_copy(tok, x_all.at[pl.ds(HEAD, ROWS), :], lsem.at[1])
    small = [pltpu.make_async_copy(src, dst, lsem.at[6 + i]) for i, (src, dst) in enumerate(
        ((taps_in, taps), (skip_in, skip), (rates_in, rates), (resid_in, resid)))]
    pairs_in = pltpu.make_async_copy(wkv_in, raw, lsem.at[0])
    pairs_in.start()
    load.start()
    for c in small:
        c.start()

    acc0[...] = jnp.zeros_like(acc0)
    acc1[...] = jnp.zeros_like(acc1)
    acc_q[...] = jnp.zeros_like(acc_q)
    pl.semaphore_wait(barrier, 11)

    class Gather:
        def __init__(self, p, src, buf, cut):
            self.p, self.src, self.buf = p, src, buf
            self.r, self.n = (raw.shape[0], buf.shape[1]) if src is None else src.shape
            self.cut = cut

        def piece(self, z, x, k, part="", half=None, flip=0):
            first = pl.multiple_of(at(z, x, k) * self.r, self.r)
            low, high = {"": (0, self.r), "A": (0, self.cut), "B": (self.cut, self.r)}[part]
            columns = slice(None)
            if half is not None and high - low < 32:
                columns = pl.ds(half * (self.n // 2), self.n // 2)
            elif half is not None:
                units = (high - low) // 16
                middle = low + (units // 2 if flip else units - units // 2) * 16
                low, high = ((low, middle), (middle, high))[half]
            return self.buf.at[pl.ds(pl.multiple_of(first + low, 16), high - low), columns]

        def put(self, ref, i, to, src=None):
            copy(ref if src is None else src, ref, send.at[self.p], recv.at[self.p, i], seq=to).start()

        def got(self, ref, i):
            copy(ref, ref, send.at[self.p], recv.at[self.p, i], seq=sib).wait_recv()

        def pair(self, dz, dx):
            self.put(self.piece(zh + dz, xx + dx, core), 24 + dx, sib)

        def S(self):
            own = self.piece(zh, xx, core)
            self.put(own, 0, zp, self.src)
            self.put(own, 1, zm, self.src)

        def T(self):
            own = self.piece(zh, xx, core)
            self.put(own, 3, xp, self.src)
            self.put(own, 4, xm, self.src)
            self.put(own, 24, sib, self.src)
            self.local = None
            if self.src is not None:
                self.local = pltpu.make_async_copy(self.src, own, lsem.at[self.p])
                self.local.start()

        def ring(self, where, base, plus, minus, d, flip):
            if d == 3:
                self.got(where(3), base)
                self.put(where(3, 0, flip), base + 2, plus)
            elif d == 1:
                self.got(where(1), base + 1)
                self.put(where(1, 1, flip), base + 2, minus)
            else:
                self.got(where(2), base + 2)

        def X(self, i):
            d = (3, 1, 2)[i]
            self.ring(lambda d, h=None, f=0: self.piece(zh, xx + d, core, "", h, f), 3, xp, xm, d, 0)
            part = self.piece(zh, xx + d, core, "B")
            self.put(part, 15 + 3 * i, zp)
            self.put(part, 16 + 3 * i, zm)
            self.pair(0, d)

        def Z(self, j):
            d = (3, 1, 2)[j]
            self.ring(lambda d, h=None, f=0: self.piece(zh + d, xx, core, "", h, f), 0, zp, zm, d, 0)
            part = self.piece(zh + d, xx, core, "A")
            self.put(part, 6 + 3 * j, xp)
            self.put(part, 7 + 3 * j, xm)
            self.pair(d, 0)

        def A(self, j, d):
            dz = (3, 1, 2)[j]
            self.ring(lambda d, h=None, f=0: self.piece(zh + dz, xx + d, core, "A", h, f),
                      6 + 3 * j, xp, xm, d, (j + self.p) % 2)

        def B(self, i, d):
            dx = (3, 1, 2)[i]
            self.ring(lambda d, h=None, f=0: self.piece(zh + d, xx + dx, core, "B", h, f),
                      15 + 3 * i, zp, zm, d, (i + self.p) % 2)

        def D(self, j, i):
            dz, dx = (3, 1, 2)[j], (3, 1, 2)[i]
            if dx == 2:
                self.A(j, 2)
            if dz == 2:
                self.B(i, 2)
            self.pair(dz, dx)

        def others(self, dx):
            self.got(self.buf.at[pl.ds(0, 4 * self.r), :], 24 + dx)

        def drain(self):
            ref = self.buf.at[pl.ds(0, 31 * self.r), :]
            copy(ref, ref, send.at[self.p], recv.at[self.p, 0], seq=sib).wait_send()

    gathers = [
        Gather(0, None, wa0, CUT_KV),
        Gather(1, None, wa1, CUT_KV),
        Gather(2, wq_in.at[:, pl.ds(0, 128)], wq0, CUT),
        Gather(3, wq_in.at[:, pl.ds(128, 128)], wq1, CUT),
        Gather(4, wo_in, wo, wo_in.shape[0] // 4 * 3),
    ]
    started = []
    sums = [(acc0, 0), (acc1, 0), (acc_q, 0), (acc_q, 128)]

    def multiply(p, dx):
        g = gathers[p]
        acc, low = sums[p]
        if not started:
            started.append(True)
            take_ends()
        if dx == 0:
            if g.local is not None:
                g.local.wait()
        g.others(dx)

        @pl.loop(0, 4, step=2)
        def _(dz):
            where = [pl.ds(pl.multiple_of(at(zh + dz + i, xx + dx, 0) * g.r, 2 * g.r), 2 * g.r) for i in range(2)]
            left = jnp.concatenate([x_all[:, w] for w in where], axis=1)
            right = jnp.concatenate([g.buf[w, :] for w in where], axis=0)
            acc[:, low:low + g.n] += jnp.dot(left, right, preferred_element_type=F32)

    def short(acc, cols, which, lanes, i):
        v = acc[pl.ds(pl.multiple_of(i * SUB + HEAD - 8, 8), SUB + 8), cols]
        return (taps[0, which:which + 1, lanes] * v[8:] + taps[1, which:which + 1, lanes] * v[7:-1]
                + taps[2, which:which + 1, lanes] * v[6:-2])

    rank8 = lax.broadcasted_iota(jnp.int32, (8, 128), 0)

    def wide(row):
        return jnp.broadcast_to(row, (8, 128))

    def total(terms):
        while len(terms) > 1:
            terms = [p + q for p, q in zip(terms[::2], terms[1::2])]
        return terms[0]

    def eput(src, dst, l, i, to):
        copy(src, dst, esend.at[l], erecv.at[l, i], seq=to).start()

    def egot(ref, l, i):
        copy(ref, ref, esend.at[l], erecv.at[l, i], seq=sib).wait_recv()

    def states(l):
        lanes = slice(l * 128, (l + 1) * 128)
        acc = sums[l][0]
        acc[0:HEAD, :] = jnp.where(seq == 0, 0.0, acc[0:HEAD, :])

        @pl.loop(0, 8)
        def _(i):
            key = short(acc, slice(0, 128), 1, lanes, i)
            value = short(acc, slice(128, 256), 2, lanes, i)
            mkv[pl.ds(pl.multiple_of(l * ROWS + i * SUB, 8), SUB), :] = key * value

        a = [wide(jnp.exp(-rates[m:m + 1, lanes])) for m in range(MODES)]
        r = [wide(resid[m:m + 1, lanes]) for m in range(MODES)]

        def step(t, hs):
            v = mkv[pl.ds(l * ROWS + t, 8, stride=SUB), :]
            hs = [a[m] * hs[m] + v for m in range(MODES)]
            conv[pl.ds(l * ROWS + t, 8, stride=SUB), :] = total([r[m] * hs[m] for m in range(MODES)])
            return tuple(hs)

        hs = lax.fori_loop(0, SUB, step, (jnp.zeros((8, 128), F32),) * MODES)
        for m in range(MODES):
            v = hs[m]
            for d in (1, 2, 4):
                factor = wide(jnp.exp(-rates[m:m + 1, lanes] * float(SUB * d)))
                v = v + jnp.where(rank8 >= d, factor * pltpu.roll(v, d, 0), 0.0)
            scan[l * MODES + m] = v
            e_own[l, m:m + 1, :] = v[7:8, :]
        eput(e_own.at[l], e_sib.at[l], l, 0, sib)

    def pairs(l):
        lam = rates[:, l * 128:(l + 1) * 128]
        e0 = jnp.where(core == 0, e_own[l], e_sib[l])
        e1 = jnp.where(core == 0, e_sib[l], e_own[l])
        return lam, jnp.exp(-lam * float(ROWS)), e0, e1

    def chip_state(l):
        egot(e_sib.at[l], l, 0)
        lam, step1, e0, e1 = pairs(l)
        c_x[l, xx] = step1 * e0 + e1
        mine = c_x.at[l, xx]
        for to in (xp, xm, xo):
            eput(mine, mine, l, 1, to)

    def row_state(l):
        lam = rates[:, l * 128:(l + 1) * 128]
        egot(c_x.at[l, pl.ds(0, 3)], l, 1)
        row = c_x[l, 3]
        for k in range(3):
            row = row + jnp.exp(-lam * float(2 * ROWS * (3 - k))) * c_x[l, k]
        r_z[l, zh] = row
        mine = r_z.at[l, zh]
        for to in (zp, zm, zo):
            eput(mine, mine, l, 2, to)

    def enter(l):
        lanes = slice(l * 128, (l + 1) * 128)
        lam, step1, e0, e1 = pairs(l)
        egot(r_z.at[l, pl.ds(0, 3)], l, 2)
        state = jnp.zeros_like(lam)
        for k in range(3):
            gap = jnp.maximum(zh - 1 - k, 0).astype(F32) * float(8 * ROWS)
            state = state + jnp.where(k < zh, jnp.exp(-lam * gap) * r_z[l, k], 0.0)
        state = jnp.exp(-lam * (xx.astype(F32) * float(2 * ROWS))) * state
        for k in range(3):
            gap = jnp.maximum(xx - 1 - k, 0).astype(F32) * float(2 * ROWS)
            state = state + jnp.where(k < xx, jnp.exp(-lam * gap) * c_x[l, k], 0.0)
        state = jnp.where(core == 0, state, e0 + step1 * state)

        a = [wide(jnp.exp(-rates[m:m + 1, lanes])) for m in range(MODES)]
        gs = []
        for m in range(MODES):
            rate = wide(rates[m:m + 1, lanes])
            first = jnp.where(rank8 >= 1, pltpu.roll(scan[l * MODES + m], 1, 0), 0.0)
            first = first + jnp.exp(-rate * (rank8.astype(F32) * float(SUB))) * wide(state[m:m + 1, :])
            gs.append(wide(resid[m:m + 1, lanes]) * a[m] * first)
        direct = wide(skip[0:1, lanes])

        def step(t, gs):
            place = pl.ds(l * ROWS + t, 8, stride=SUB)
            conv[place, :] = conv[place, :] + total(list(gs)) + direct * mkv[place, :]
            return tuple(a[m] * gs[m] for m in range(MODES))

        lax.fori_loop(0, SUB, step, tuple(gs))

    def gref(c, l, q, half=None):
        rows = ROWS // 2 if half is None else ROWS // 4
        return gate.at[c * 2 + l, pl.ds(q * (ROWS // 2) + (half or 0) * rows, rows), :]

    def gput(ref, l, q, i, to):
        copy(ref, ref, gsend.at[l], grecv.at[l, q, i], chan=to).start()

    def ggot(ref, l, q, i):
        copy(ref, ref, gsend.at[l], grecv.at[l, q, i], chan=lp).wait_recv()

    def gating(l, q):
        lanes = slice(l * 128, (l + 1) * 128)
        if q == 0:
            acc_q[0:HEAD, lanes] = jnp.where(seq == 0, 0.0, acc_q[0:HEAD, lanes])
        mine = gate.at[chan * 2 + l]

        @pl.loop(4 * q, 4 * q + 4)
        def _(i):
            query = short(acc_q, lanes, 0, lanes, i)
            done = query * conv[pl.ds(pl.multiple_of(l * ROWS + i * SUB, 8), SUB), :]
            mine[pl.ds(pl.multiple_of(i * SUB, 16), SUB), :] = done.astype(BF16)

        ref = gref(chan, l, q)
        gput(ref, l, q, 0, lp)
        gput(ref, l, q, 1, yp)
        gput(ref, l, q, 2, ym)

    def gate_pair(l, q):
        ref = gref(lp, l, q)
        ggot(ref, l, q, 0)
        gput(ref, l, q, 3, yp)
        gput(ref, l, q, 4, ym)

    def gate_ring(l, q, j, d):
        side = zl if j == 0 else 1 - zl
        ref = gref(cat(yy + d, side), l, q)
        if d == 3:
            ggot(ref, l, q, 1 + 2 * j)
            gput(gref(cat(yy + 3, side), l, q, 0), l, q, 5 + j, yp)
        elif d == 1:
            ggot(ref, l, q, 2 + 2 * j)
            gput(gref(cat(yy + 1, side), l, q, 1), l, q, 5 + j, ym)
        else:
            ggot(ref, l, q, 5 + j)

    def project(l):
        if l == 0:
            for dx in range(4):
                gathers[4].others(dx)
            gathers[4].local.wait()
        for q in range(2):
            for j in range(2):
                gate_ring(l, q, j, 2)

        @pl.loop(0, out.shape[1] // 256)
        def _(n):
            columns = pl.ds(pl.multiple_of(n * 256, 256), 256)
            left = jnp.concatenate([gate[2 * i + l] for i in range(8)], axis=1)
            right = jnp.concatenate([wo[i * 256 + l * 128:i * 256 + l * 128 + 128, columns] for i in range(8)], axis=0)
            part = jnp.dot(left, right, preferred_element_type=F32)
            if l == 0:
                acc_o[:, columns] = part
            else:
                held[:, columns] = (acc_o[:, columns] + part).astype(BF16)
                pltpu.make_async_copy(held.at[:, columns], out.at[:, columns], osem.at[n]).start()

    tail = copy(ends.at[0], ends.at[1], tsem.at[0], tsem.at[1], seq=following)
    parts = x_all.shape[1] // 8
    rank16 = lax.broadcasted_iota(jnp.int32, (HEAD, parts), 0)

    def rows_apart():
        pairs_in.wait()
        apart = jnp.swapaxes(raw[...], 0, 1)
        mine = pl.ds(pl.multiple_of(seq * raw.shape[0], raw.shape[0]), raw.shape[0])
        for l, ref in enumerate((wa0, wa1)):
            for which in range(2):
                ref[mine, which * 128:(which + 1) * 128] = apart[which, :, l * 128:(l + 1) * 128]

    def send_ends():
        load.wait()
        for c in small:
            c.wait()
        packed = jnp.zeros((HEAD, parts), F32)
        for i in range(8):
            rows = x_all[ROWS:ROWS + HEAD, i * parts:(i + 1) * parts].astype(F32)
            packed = jnp.where(rank16 // 2 == i, pltpu.roll(rows, (2 * i + 2) % HEAD, 0), packed)
        ends[0] = packed.astype(BF16)
        tail.start()

    def take_ends():
        tail.wait_recv()
        packed = ends[1].astype(F32)
        for i in range(8):
            rows = packed if i == 7 else pltpu.roll(packed, HEAD - 2 - 2 * i, 0)
            x_all[0:HEAD, i * parts:(i + 1) * parts] = rows.astype(BF16)


    actions = {"RL": rows_apart, "E": send_ends, "C": states, "E1": chip_state, "E2": row_state, "E3": enter,
               "GT": gating, "GL": gate_pair, "OUT": project}
    for name in ORDER:
        if "." not in name:
            if name[:2] == "GY":
                gate_ring(int(name[2]), int(name[3]), int(name[4]), 3 if name[5] == "-" else 1)
            else:
                what = name.rstrip("01")
                if name[:2] in ("E1", "E2", "E3"):
                    what = name[:2]
                actions[what](*[int(c) for c in name[len(what):]])
            continue
        g, what = gathers[int(name[0])], name[2:]
        kind = what[0]
        if kind == "M":
            multiply(g.p, int(what[1]))
        elif kind in "ST":
            getattr(g, kind)()
        elif kind in "XZ":
            getattr(g, kind)(int(what[1]) - 1)
        elif kind == "D":
            g.D(int(what[1]), int(what[2]))
        else:
            getattr(g, kind)(int(what[1]), 3 if what[2] == "-" else 1)

    for g in gathers:
        g.drain()
    tail.wait_send()

    @pl.loop(0, out.shape[1] // 256)
    def _(n):
        columns = pl.ds(pl.multiple_of(n * 256, 256), 256)
        pltpu.make_async_copy(held.at[:, columns], out.at[:, columns], osem.at[n]).wait()

    for l in range(2):
        ref = mkv.at[pl.ds(0, 7 * MODES), :]
        copy(ref, ref, esend.at[l], erecv.at[l, 0], seq=sib).wait_send()
        ref = gate.at[pl.ds(0, 7)]
        copy(ref, ref, gsend.at[l], grecv.at[l, 0, 0], chan=lp).wait_send()


def shards(tokens, w_query, w_keyval, short_taps, skip_gain, decay_rates, residues, w_output):
    depth, _, width = w_keyval.shape
    hbm = pl.BlockSpec(memory_space=pl.ANY)
    dma = pltpu.SemaphoreType.DMA
    model = tokens.shape[1]
    return pl.pallas_call(
        kernel,
        out_shape=jax.ShapeDtypeStruct((ROWS, w_output.shape[1]), BF16),
        in_specs=[hbm] * 8,
        out_specs=hbm,
        scratch_shapes=[
            pltpu.VMEM((HEAD + ROWS, model), BF16),
            pltpu.VMEM((model, width), BF16),
            pltpu.VMEM((model, width), BF16),
            pltpu.VMEM((model, width // 2), BF16),
            pltpu.VMEM((model, width // 2), BF16),
            pltpu.VMEM((8 * width, w_output.shape[1]), BF16),
            pltpu.VMEM((HEAD + ROWS, width), F32),
            pltpu.VMEM((HEAD + ROWS, width), F32),
            pltpu.VMEM((HEAD + ROWS, width), F32),
            pltpu.VMEM((2 * ROWS, 128), F32),
            pltpu.VMEM((2 * ROWS, 128), F32),
            pltpu.VMEM((2 * MODES, 8, 128), F32),
            pltpu.VMEM((2, MODES, 128), F32),
            pltpu.VMEM((2, MODES, 128), F32),
            pltpu.VMEM((2, 4, MODES, 128), F32),
            pltpu.VMEM((2, 4, MODES, 128), F32),
            pltpu.VMEM((16, ROWS, 128), BF16),
            pltpu.VMEM((ROWS, w_output.shape[1]), F32),
            pltpu.VMEM((2, HEAD, model // 8), BF16),
            pltpu.VMEM((3, 3, width), F32),
            pltpu.VMEM((1, width), F32),
            pltpu.VMEM((MODES, width), F32),
            pltpu.VMEM((MODES, width), F32),
            pltpu.VMEM((depth, 2, width), BF16),
            pltpu.VMEM((ROWS, w_output.shape[1]), BF16),
            dma((5,)), dma((5, 28)),
            dma((2,)), dma((2, 3)),
            dma((2,)), dma((2, 2, 7)),
            dma((10,)), dma((2,)), dma((4,)),
        ],
        compiler_params=pltpu.CompilerParams(
            collective_id=0, has_side_effects=True, vmem_limit_bytes=56 * 1024 * 1024),
        cost_estimate=pl.CostEstimate(flops=2 * ROWS * model * 4 * width, bytes_accessed=2 * ROWS * model, transcendentals=0),
    )(tokens, w_keyval, w_query, w_output, short_taps, skip_gain[None, :],
      decay_rates.T, residues.T)


def solution(mesh):
    return jax.shard_map(
        shards,
        mesh=mesh,
        in_specs=(
            P("seq", None),
            P("seq", "chan"),
            P("seq", None, "chan"),
            P(None, None, "chan"),
            P("chan"),
            P("chan", None),
            P("chan", None),
            P("seq", "chan"),
        ),
        out_specs=P("seq", "chan"),
        check_vma=False,
    )
```
